256 devices in a mesh: dp: 64 (over z, y, core), expert: 4 (over x).
Axes of the slice: x: 4, y: 4, z: 8, core: 2. Of those that a mesh axis runs over, the one named last changes fastest.
Arguments:
- gradient: bfloat16 [4, 64, 64, 4096], P('expert', None, 'dp'), may hold values from -4000 to 4000
- second_moment: float32 [4, 64, 64, 4096], P('expert', None, 'dp'), may hold values from 0.1 to 10
- left_stat: float32 [4, 64, 512, 512], P('expert', 'dp'), may hold values from -4 to 4
- right_stat: float32 [4, 64, 512, 512], P('expert', 'dp'), may hold values from -4 to 4
- left_root: float32 [4, 64, 512, 512], P('expert', 'dp'), may hold values from -1 to 3
- right_root: float32 [4, 64, 512, 512], P('expert', 'dp'), may hold values from -1 to 3
- owner_table: int32 [4, 64], P('expert'), may hold values from 0 to 63, each once within a row
Outputs:
- update: bfloat16 [4, 64, 64, 4096], P('expert', None, 'dp')
- moment_new: float32 [4, 64, 64, 4096], P('expert', None, 'dp')
- left_new: float32 [4, 64, 512, 512], P('expert', 'dp')
- right_new: float32 [4, 64, 512, 512], P('expert', 'dp')
The draws below stay inside these ranges and needn't reach their ends.
Inputs may be any that keep to these rules, and one draw needn't show every extreme that they name: Each row is a permutation; block b of expert e is held by dp index owner_table[e, b].
All inputs are finite; a program needn't handle non-finite values.
Results may differ from the reference program's by a relative error of at most 0.0049.
Values may be sent and summed in bfloat16 or wider, within the bound.
No kernel may reach another device: no remote copies, remote signals or barrier semaphores. Data moves between devices by JAX's collectives and lax.ppermute only.
A program may use at most 64 MiB of HBM per device.

```python
import math
import jax
import jax.numpy as jnp
from jax import lax

D = 4096
H = 4096
BLOCK = 512
EXPERTS = 4
QROWS = 64
NBLK = 64
N_DP = 64


def draw_gradient(key, part):
    key = jax.random.fold_in(key, 11)
    key_rows, key_cols, key_base = jax.random.split(key, 3)
    shape = (EXPERTS, QROWS, N_DP, H)
    row_span = math.log(10.0)
    base = jax.random.truncated_normal(key_base, -4.0, 4.0, shape, jnp.float32)
    rows = jnp.exp(jax.random.uniform(key_rows, (EXPERTS, QROWS, N_DP, 1), jnp.float32, 0.0, row_span))
    cols = jnp.exp(jax.random.uniform(key_cols, (EXPERTS, 1, 1, H), jnp.float32, 0.0, math.log(10.0)))
    ramp_dp = 3.0 ** (jnp.arange(N_DP, dtype=jnp.float32) / max(N_DP - 1, 1))
    ramp_expert = 1.0 + 0.5 * jnp.arange(EXPERTS, dtype=jnp.float32) / max(EXPERTS - 1, 1)
    ramp = ramp_expert.reshape(EXPERTS, 1, 1, 1) * ramp_dp.reshape(1, 1, N_DP, 1)
    return (base * rows * cols * ramp).astype(jnp.bfloat16)


def root_matrix(key, off_scale):
    key_off, key_diag = jax.random.split(key, 2)
    shape = (EXPERTS, NBLK, BLOCK, BLOCK)
    off = jax.random.truncated_normal(key_off, -4.0, 4.0, shape, jnp.float32) * off_scale
    diag = jnp.exp(jax.random.uniform(key_diag, (EXPERTS, NBLK, BLOCK, 1), jnp.float32, math.log(0.5), math.log(2.0)))
    same = (jnp.arange(BLOCK)[:, None] == jnp.arange(BLOCK)[None, :]).astype(jnp.float32)
    return off + same * diag


def draw_left_root(key, part):
    key = jax.random.fold_in(key, 21)
    return root_matrix(key, 0.5 / math.sqrt(BLOCK))


def draw_right_root(key, part):
    key = jax.random.fold_in(key, 22)
    return root_matrix(key, 0.5 / math.sqrt(BLOCK))


def block_levels(stream_key, extent, cuts, least, largest):
    def one(dim, parts):
        draws = jax.random.uniform(jax.random.fold_in(jax.random.fold_in(stream_key, 6), dim), (parts,), jnp.float32, least / len(cuts), largest / len(cuts))
        return jnp.repeat(jnp.exp(draws), extent[dim] // parts).reshape((-1,) + (1,) * (len(extent) - dim - 1))

    factor_of = one(*cuts[0])
    for cut in cuts[1:]:
        factor_of = factor_of * one(*cut)
    return factor_of


def scatter_about(stream_key, shape, deviation, most, cuts=(), kind=jnp.bfloat16):
    level = block_levels(stream_key, shape, cuts, -0.22, 0.18) if cuts else 1.0
    array = jax.random.normal(stream_key, shape, jnp.float32) * deviation * level
    return jnp.minimum(jnp.maximum(array, -most), most).astype(kind)


def setup_inputs(seed: int = 0) -> dict:
    streams_of = jax.random.split(jax.random.key(seed), 8)
    gradient = draw_gradient(jax.random.fold_in(streams_of[7], 71), 0)
    second_moment = jnp.clip(jnp.exp(math.log(10.0) - 4.6051702 * jax.random.uniform(streams_of[1], (EXPERTS, QROWS, N_DP, H), jnp.float32) ** block_levels(streams_of[1], (EXPERTS, QROWS, N_DP, H), ((0, 4), (2, 64)), -0.2, 0.2)), 0.1, 10.0)
    left_stat = scatter_about(streams_of[2], (EXPERTS, NBLK, BLOCK, BLOCK), 0.5, 4.0, ((0, 4), (1, 64)), jnp.float32)
    right_stat = scatter_about(streams_of[3], (EXPERTS, NBLK, BLOCK, BLOCK), 0.5, 4.0, ((0, 4), (1, 64)), jnp.float32)
    left_root = draw_left_root(jax.random.fold_in(streams_of[7], 71), 0)
    right_root = draw_right_root(jax.random.fold_in(streams_of[7], 71), 0)
    owner_table = jax.vmap(lambda own: jax.random.permutation(own, NBLK))(jax.random.split(streams_of[6], EXPERTS)).reshape((EXPERTS, NBLK)).astype(jnp.int32)
    return dict(gradient=gradient, second_moment=second_moment, left_stat=left_stat, right_stat=right_stat, left_root=left_root, right_root=right_root, owner_table=owner_table)


STAT_DECAY = 0.9
MOMENT_DECAY = 0.99
ADAM_EPS = 1e-08
NORM_EPS = 1e-06

def reference(gradient, second_moment, left_stat, right_stat, left_root, right_root, owner_table):
    grad_wide = gradient.astype(jnp.float32)
    grad_sq = jnp.sum(grad_wide * grad_wide)
    norm_limit = math.sqrt(EXPERTS * D * H)
    clip_factor = norm_limit / jnp.maximum(jnp.sqrt(grad_sq), norm_limit)
    clipped = clip_factor * grad_wide
    moment = MOMENT_DECAY * second_moment + (1.0 - MOMENT_DECAY) * clipped * clipped
    adam_dir = clipped / (jnp.sqrt(moment) + ADAM_EPS)
    row_blocks = D // BLOCK
    col_blocks = H // BLOCK
    total_blocks = row_blocks * col_blocks
    gram_weight = (1.0 - STAT_DECAY) * clip_factor * clip_factor / BLOCK

    def one_block(item):
        piece, left_old, right_old, left_inv, right_inv, adam_sq = item
        left_next = STAT_DECAY * left_old + gram_weight * jnp.dot(piece, piece.T, preferred_element_type=jnp.float32)
        right_next = STAT_DECAY * right_old + gram_weight * jnp.dot(piece.T, piece, preferred_element_type=jnp.float32)
        shampoo_f = jnp.dot(left_inv, piece.astype(jnp.float32), precision=lax.Precision.HIGHEST)
        shampoo_f = jnp.dot(shampoo_f, right_inv, precision=lax.Precision.HIGHEST)
        shampoo_sq = jnp.sum(shampoo_f * shampoo_f)
        shampoo = lax.optimization_barrier(shampoo_f.astype(jnp.bfloat16))
        graft_ratio = jnp.sqrt(adam_sq) / jnp.sqrt(shampoo_sq + NORM_EPS)
        final = (graft_ratio * shampoo.astype(jnp.float32)).astype(jnp.bfloat16)
        return (left_next, right_next, final)
    updates = []
    lefts = []
    rights = []
    for expert_id in range(EXPERTS):
        full = gradient[expert_id].reshape(D, H)
        blocks = full.reshape(row_blocks, BLOCK, col_blocks, BLOCK).transpose(0, 2, 1, 3).reshape(total_blocks, BLOCK, BLOCK)
        adam_full = adam_dir[expert_id].reshape(D, H)
        adam_sq = lax.optimization_barrier(jnp.sum((adam_full * adam_full).reshape(row_blocks, BLOCK, col_blocks, BLOCK), axis=(1, 3))).reshape(total_blocks)
        owners = owner_table[expert_id].astype(jnp.int32)
        block_of = jnp.zeros((total_blocks,), jnp.int32).at[owners].set(jnp.arange(total_blocks, dtype=jnp.int32))
        left_next, right_next, finals = lax.map(one_block, (blocks[block_of], left_stat[expert_id], right_stat[expert_id], left_root[expert_id], right_root[expert_id], adam_sq[block_of]))
        by_block = finals[owners]
        updates.append(by_block.reshape(row_blocks, col_blocks, BLOCK, BLOCK).transpose(0, 2, 1, 3).reshape(QROWS, N_DP, H))
        lefts.append(left_next)
        rights.append(right_next)
    return (jnp.stack(updates), moment, jnp.stack(lefts), jnp.stack(rights))
```

```python
import functools
import math

import jax
import jax.numpy as jnp
from jax import lax
from jax.experimental import pallas as pl
from jax.experimental.pallas import tpu as pltpu
from jax.sharding import PartitionSpec as P

STAT_DECAY = 0.9
MOMENT_DECAY = 0.99
ADAM_EPS = 1e-08
NORM_EPS = 1e-06
LANES = 128
SUB = 8
F32 = jnp.float32
BF16 = jnp.bfloat16
VMEM_LIMIT = 48 * 1024 * 1024


def call(body, out_shape, in_specs, out_specs, name, flops=0, moved=0, **kw):
    return pl.pallas_call(
        body,
        out_shape=out_shape,
        in_specs=in_specs,
        out_specs=out_specs,
        name=name,
        compiler_params=pltpu.CompilerParams(vmem_limit_bytes=VMEM_LIMIT),
        cost_estimate=pl.CostEstimate(flops=flops, bytes_accessed=moved, transcendentals=0),
        **kw,
    )


def vmem():
    return pl.BlockSpec(memory_space=pltpu.VMEM)


def smem():
    return pl.BlockSpec(memory_space=pltpu.SMEM)


def dot(a, b, ca=1, cb=0):
    return lax.dot_general(a, b, (((ca,), (cb,)), ((), ())), preferred_element_type=F32)


def split2(x):
    high = x.astype(BF16)
    return high, (x - high.astype(F32)).astype(BF16)


def spread(x):
    high = x.astype(BF16).astype(F32)
    rest = x - high
    mid = rest.astype(BF16).astype(F32)
    low = rest - mid
    row = lax.broadcasted_iota(jnp.int32, x.shape, 0)
    return jnp.where(row == 0, high, jnp.where(row == 1, mid, jnp.where(row == 2, low, 0.0))).astype(BF16)


def clip_of(grad_sq, limit):
    return limit / jnp.maximum(jnp.sqrt(grad_sq), limit)


def pack_kernel(row_blocks, col_blocks, block, owners, grad, out):
    total = jnp.zeros((SUB, block), F32)
    for pair in range(0, row_blocks, 2):
        for col in range(col_blocks):
            wide = grad[pair * SUB : (pair + 2) * SUB, col * block : (col + 1) * block].astype(F32)
            for half in range(2):
                piece = wide[half * SUB : (half + 1) * SUB]
                total += piece * piece
                out[owners[(pair + half) * col_blocks + col], :, :block] = piece.astype(BF16)
    tile = jnp.broadcast_to(jnp.sum(total, keepdims=True), (SUB, LANES))
    out[:, :, block:] = jnp.broadcast_to(spread(tile)[None], (out.shape[0], SUB, LANES))


def gather_sum_kernel(tiles, out):
    wide = tiles[...].astype(F32)
    out[...] = jnp.sum(jnp.sum(wide, axis=0), axis=0, keepdims=True)


def roots_kernel(dp, left, right, l_high, l_low, r_high, r_low):
    n = left.shape[0]
    row = lax.broadcasted_iota(jnp.int32, (n, n), 0)
    col = lax.broadcasted_iota(jnp.int32, (n, n), 1)
    per = n // dp
    order = (col == (row % per) * dp + row // per).astype(BF16)
    high, low = split2(left[...])
    for part, dest in ((high, l_high), (low, l_low)):
        rows = dot(order, part).astype(BF16)
        dest[...] = dot(rows, order, 1, 1).astype(BF16)
    r_high[...], r_low[...] = split2(right[...])


def left_kernel(l_high, l_low, arrived, piece, half):
    block = piece.shape[1]
    wide = arrived[:, :, :block].astype(F32).reshape(piece.shape)
    piece[...] = wide.astype(BF16)
    g = piece[...]
    half[...] = dot(l_high[...], g) + dot(l_low[...], g)


def right_kernel(half, r_high, r_low, out, norm):
    block = half.shape[1]
    high, low = split2(half[...])
    full = dot(high, r_high[...]) + dot(high, r_low[...]) + dot(low, r_high[...])
    norm[...] = jnp.broadcast_to(jnp.sum(full * full, keepdims=True), norm.shape)
    out[:, :, :block] = full.reshape(out.shape[0], SUB, block).astype(BF16)


def adam_kernel(limit, row_blocks, col_blocks, block, grad, second, sq_a, sq_b, norm, _, moment, tail, parts):
    clip = clip_of(sq_a[...] + sq_b[...], limit)
    chunks = block // LANES
    wide_chunks = col_blocks * chunks
    parts[...] = jnp.zeros_like(parts)
    for pair in range(0, row_blocks, 2):
        for col in range(col_blocks):
            sums = [jnp.zeros((SUB, LANES), F32) for _ in range(2)]
            for chunk in range(chunks):
                k = col * chunks + chunk
                wide = grad[pair * SUB : (pair + 2) * SUB, k * LANES : (k + 1) * LANES].astype(F32)
                for half in range(2):
                    clipped = clip * wide[half * SUB : (half + 1) * SUB]
                    place = pl.ds((pair + half) * SUB * wide_chunks + k, SUB, stride=wide_chunks)
                    new = MOMENT_DECAY * second[place, :] + (1.0 - MOMENT_DECAY) * clipped * clipped
                    moment[place, :] = new
                    adam = clipped / (jnp.sqrt(new) + ADAM_EPS)
                    sums[half] += adam * adam
            for half in range(2):
                b = (pair + half) * col_blocks + col
                parts[b : b + 1, :] = jnp.sum(sums[half], axis=0, keepdims=True)
    sums = lax.dot_general(
        jnp.ones((SUB, LANES), F32),
        parts[...],
        (((1,), (1,)), ((), ())),
        precision=lax.Precision.HIGHEST,
        preferred_element_type=F32,
    )
    lane = lax.broadcasted_iota(jnp.int32, (SUB, LANES), 1)
    tile = jnp.where(lane == row_blocks * col_blocks, norm[...], sums)
    tail[...] = jnp.broadcast_to(spread(tile)[None], tail.shape)


def gram_kernel(limit, dp, piece, left, right, sq_a, sq_b, left_new, right_new):
    n = piece.shape[0]
    clip = clip_of(sq_a[:, :1] + sq_b[:, :1], limit)
    weight = (1.0 - STAT_DECAY) * clip * clip / n
    row = lax.broadcasted_iota(jnp.int32, (n, n), 0)
    col = lax.broadcasted_iota(jnp.int32, (n, n), 1)
    per = n // dp
    order = (row == (col % per) * dp + col // per).astype(BF16)
    g = piece[...]
    right_new[...] = STAT_DECAY * right[...] + weight * dot(g, g, 0, 0)
    g = dot(order, g).astype(BF16)
    left_new[...] = STAT_DECAY * left[...] + weight * dot(g, g, 1, 1)


def place_kernel(row_blocks, col_blocks, block, owners, owner_lanes, returned, update):
    blocks = row_blocks * col_blocks
    tiles = jnp.sum(returned[:, :, block:].astype(F32), axis=1)
    adam_sq = jnp.sum(tiles, axis=0, keepdims=True)[:, :blocks]
    slot = lax.broadcasted_iota(jnp.int32, (tiles.shape[0], blocks), 0)
    norms = jnp.where(owner_lanes[...] == slot, tiles[:, blocks : blocks + 1], 0.0)
    norm_sq = jnp.sum(norms, axis=0, keepdims=True)
    ratio = jnp.sqrt(adam_sq) / jnp.sqrt(norm_sq + NORM_EPS)
    for pair in range(0, row_blocks, 2):
        for col in range(col_blocks):
            rows = []
            for half in range(2):
                b = (pair + half) * col_blocks + col
                rows.append(ratio[:, b : b + 1] * returned[owners[b], :, :block].astype(F32))
            update[pair * SUB : (pair + 2) * SUB, col * block : (col + 1) * block] = jnp.concatenate(
                rows, axis=0
            ).astype(BF16)


def on_device(gradient, second_moment, left_stat, right_stat, left_root, right_root, owner_table):
    dp = lax.axis_size("dp")
    experts = lax.axis_size("expert")
    _, local_rows, _, width = gradient.shape
    block = left_stat.shape[-1]
    row_blocks = local_rows // SUB
    col_blocks = width // block
    limit = math.sqrt(experts * local_rows * dp * width)
    grid = (row_blocks, col_blocks, block)
    grad = gradient.reshape(local_rows, width)
    second = second_moment.reshape(local_rows * width // LANES, LANES)
    owners = owner_table[0]
    packed = jax.ShapeDtypeStruct((dp, SUB, block + LANES), BF16)
    square = functools.partial(jax.ShapeDtypeStruct, (block, block))
    line = jax.ShapeDtypeStruct((1, LANES), F32)
    cube = 2 * block**3
    area = block * block

    def exchange(x):
        return lax.all_to_all(x, "dp", split_axis=0, concat_axis=0, tiled=True)

    outgoing = call(
        functools.partial(pack_kernel, *grid), packed, [smem(), vmem()], vmem(), "pack", moved=4 * area
    )(owners, grad)
    arrived = exchange(outgoing)
    l_high, l_low, r_high, r_low = call(
        functools.partial(roots_kernel, dp),
        (square(BF16),) * 4,
        [vmem()] * 2,
        (vmem(),) * 4,
        "roots",
        flops=4 * cube,
        moved=16 * area,
    )(left_root[0, 0], right_root[0, 0])
    tail = pl.BlockSpec((dp, SUB, LANES), lambda _: (0, 0, block // LANES))
    sq_a = call(gather_sum_kernel, line, [tail], vmem(), "norm", moved=area, grid=(1,))(arrived)
    sq_b = lax.ppermute(sq_a, "expert", [(j, j ^ 1) for j in range(experts)])
    piece, half = call(
        left_kernel, (square(BF16), square(F32)), [vmem()] * 3, (vmem(),) * 2, "left", flops=2 * cube, moved=12 * area
    )(l_high, l_low, arrived)
    sq_a = sq_a + sq_b
    sq_b = lax.ppermute(sq_a, "expert", [(j, j ^ 2) for j in range(experts)])
    ready, norm = call(
        right_kernel,
        (packed, jax.ShapeDtypeStruct((SUB, LANES), F32)),
        [vmem()] * 3,
        (vmem(),) * 2,
        "right",
        flops=3 * cube,
        moved=10 * area,
    )(half, r_high, r_low)
    moment, ready = call(
        functools.partial(adam_kernel, limit, *grid),
        (jax.ShapeDtypeStruct(second.shape, F32), packed),
        [vmem()] * 5 + [pl.BlockSpec(memory_space=pl.ANY)],
        (vmem(), tail),
        "adam",
        moved=10 * area,
        scratch_shapes=[pltpu.VMEM((LANES, LANES), F32)],
        input_output_aliases={5: 1},
        grid=(1,),
    )(grad, second, sq_a, sq_b, norm, ready)
    returned = exchange(ready)
    left_new, right_new = call(
        functools.partial(gram_kernel, limit, dp),
        (square(F32),) * 2,
        [vmem()] * 5,
        (vmem(),) * 2,
        "gram",
        flops=3 * cube,
        moved=18 * area,
    )(piece, left_stat[0, 0], right_stat[0, 0], sq_a, sq_b)
    update = call(
        functools.partial(place_kernel, *grid),
        jax.ShapeDtypeStruct((local_rows, width), BF16),
        [smem(), vmem(), vmem()],
        vmem(),
        "place",
        moved=4 * area,
    )(owners, owner_table, returned)
    return (
        update.reshape(gradient.shape),
        moment.reshape(second_moment.shape),
        left_new[None, None],
        right_new[None, None],
    )


def solution(mesh):
    rows = P("expert", None, "dp", None)
    slots = P("expert", "dp", None, None)
    return jax.shard_map(
        on_device,
        mesh=mesh,
        in_specs=(rows, rows, slots, slots, slots, slots, P("expert", None)),
        out_specs=(rows, rows, slots, slots),
        check_vma=False,
    )
```

```python
import functools
import math

import jax
import jax.numpy as jnp
from jax import lax
from jax.experimental import pallas as pl
from jax.experimental.pallas import tpu as pltpu
from jax.sharding import PartitionSpec as P

STAT_DECAY = 0.9
MOMENT_DECAY = 0.99
ADAM_EPS = 1e-08
NORM_EPS = 1e-06
LANES = 128
SUB = 8
ROWS = 2
FOLDS = SUB // ROWS
F32 = jnp.float32
BF16 = jnp.bfloat16
VMEM_LIMIT = 48 * 1024 * 1024
PACK_LIMIT = 64 * 1024 * 1024 - 256 * 1024


def call(body, out_shape, in_specs, out_specs, name, flops=0, moved=0, limit=VMEM_LIMIT, **kw):
    return pl.pallas_call(
        body,
        out_shape=out_shape,
        in_specs=in_specs,
        out_specs=out_specs,
        name=name,
        compiler_params=pltpu.CompilerParams(vmem_limit_bytes=limit),
        cost_estimate=pl.CostEstimate(flops=flops, bytes_accessed=moved, transcendentals=0),
        **kw,
    )


def vmem():
    return pl.BlockSpec(memory_space=pltpu.VMEM)


def smem():
    return pl.BlockSpec(memory_space=pltpu.SMEM)


def hbm():
    return pl.BlockSpec(memory_space=pltpu.HBM)


def dot(a, b, ca=1, cb=0):
    return lax.dot_general(a, b, (((ca,), (cb,)), ((), ())), preferred_element_type=F32)


def split2(x):
    high = x.astype(BF16)
    return high, (x - high.astype(F32)).astype(BF16)


def spread(x):
    high = x.astype(BF16).astype(F32)
    row = lax.broadcasted_iota(jnp.int32, x.shape, 0)
    return jnp.where(row == 0, high, x - high).astype(BF16)


def fold(x):
    return jnp.concatenate([x[:, i * ROWS : (i + 1) * ROWS] for i in range(FOLDS)], axis=2).astype(BF16)


def unfold(x, block):
    return jnp.concatenate([x[:, :, i * block : (i + 1) * block].astype(F32) for i in range(FOLDS)], axis=1)


def clip_of(grad_sq, limit):
    return limit / jnp.maximum(jnp.sqrt(grad_sq), limit)


def pack_kernel(row_blocks, col_blocks, block, table, grad, out, owners, held, ready, sems, out_sems):
    rows = 2 * SUB
    place = pltpu.make_async_copy(table, owners, sems.at[row_blocks // 2])
    place.start()
    copies = []
    for pair in range(row_blocks // 2):
        span = pl.ds(pair * rows, rows)
        copies.append(pltpu.make_async_copy(grad.at[span], held.at[span], sems.at[pair]))
        copies[-1].start()
    place.wait()
    total = jnp.zeros((SUB, block), F32)
    for pair, copy in enumerate(copies):
        copy.wait()
        for col in range(col_blocks):
            wide = held[pair * rows : (pair + 1) * rows, col * block : (col + 1) * block].astype(F32)
            for side in range(2):
                piece = wide[side * SUB : (side + 1) * SUB]
                total += piece * piece
                slot = owners[0, (2 * pair + side) * col_blocks + col]
                ready[slot, :, : FOLDS * block] = fold(piece[None])[0]
                pltpu.make_async_copy(
                    ready.at[slot, :, : FOLDS * block], out.at[slot, :, : FOLDS * block], out_sems.at[0]
                ).start()
    tile = jnp.broadcast_to(jnp.sum(total, keepdims=True), (ROWS, LANES))
    ready[:, :, FOLDS * block :] = jnp.broadcast_to(spread(tile)[None], (ready.shape[0], ROWS, LANES))
    tails = pltpu.make_async_copy(ready.at[:, :, FOLDS * block :], out.at[:, :, FOLDS * block :], out_sems.at[1])
    tails.start()
    pltpu.make_async_copy(ready.at[:, :, : FOLDS * block], out.at[:, :, : FOLDS * block], out_sems.at[0]).wait()
    tails.wait()


def sum_kernel(tiles, out):
    wide = jnp.sum(tiles[...].astype(F32), axis=0)
    out[...] = jnp.sum(wide, axis=0, keepdims=True)


def roots_kernel(dp, left, right, l_parts, r_parts):
    n = left.shape[0]
    row = lax.broadcasted_iota(jnp.int32, (n, n), 0)
    col = lax.broadcasted_iota(jnp.int32, (n, n), 1)
    per = n // dp
    order = (col == (row % per) * dp + row // per).astype(BF16)
    for i, part in enumerate(split2(left[...])):
        rows = dot(order, part).astype(BF16)
        l_parts[i] = dot(rows, order, 1, 1).astype(BF16)
    r_parts[0], r_parts[1] = split2(right[...])


def arrived_block(block, arrived):
    return unfold(arrived, block).reshape(block, block).astype(BF16)


def left_kernel(block, l_parts, arrived, half):
    g = arrived_block(block, arrived)
    half[...] = dot(l_parts[0], g) + dot(l_parts[1], g)


def right_kernel(half, r_parts, out, norm):
    block = half.shape[1]
    high, low = split2(half[...])
    full = dot(high, r_parts[0]) + dot(high, r_parts[1]) + dot(low, r_parts[0])
    norm[...] = jnp.broadcast_to(jnp.sum(full * full, keepdims=True), norm.shape)
    out[:, :, : FOLDS * block] = fold(full.reshape(out.shape[0], SUB, block))


def adam_kernel(limit, row_blocks, col_blocks, block, grad, second, sq_a, sq_b, norm, _, tail, parts):
    clip = clip_of(sq_a[...] + sq_b[...], limit)
    chunks = block // LANES
    wide_chunks = col_blocks * chunks
    parts[...] = jnp.zeros_like(parts)
    for pair in range(0, row_blocks, 2):
        for col in range(col_blocks):
            sums = [jnp.zeros((SUB, LANES), F32) for _ in range(2)]
            for chunk in range(chunks):
                k = col * chunks + chunk
                wide = grad[pair * SUB : (pair + 2) * SUB, k * LANES : (k + 1) * LANES].astype(F32)
                for side in range(2):
                    clipped = clip * wide[side * SUB : (side + 1) * SUB]
                    square = clipped * clipped
                    place = pl.ds((pair + side) * SUB * wide_chunks + k, SUB, stride=wide_chunks)
                    new = MOMENT_DECAY * second[place, :] + (1.0 - MOMENT_DECAY) * square
                    below = new * lax.rsqrt(new) + ADAM_EPS
                    sums[side] += square / (below * below)
            for side in range(2):
                b = (pair + side) * col_blocks + col
                parts[b : b + 1, :] = jnp.sum(sums[side], axis=0, keepdims=True)
    sums = lax.dot_general(
        jnp.ones((SUB, LANES), F32),
        parts[...],
        (((1,), (1,)), ((), ())),
        precision=lax.Precision.HIGHEST,
        preferred_element_type=F32,
    )
    lane = lax.broadcasted_iota(jnp.int32, (ROWS, LANES), 1)
    tile = jnp.where(lane == row_blocks * col_blocks, norm[:ROWS], sums[:ROWS])
    tail[...] = jnp.broadcast_to(spread(tile)[None], tail.shape)


def finish_kernel(limit, dp, block, wide_chunks, arrived, sq_a, sq_b, left, right, grad, second, left_new, right_new, moment):
    clip = clip_of(sq_a[...] + sq_b[...], limit)
    weight = (1.0 - STAT_DECAY) * clip[:, :1] * clip[:, :1] / block
    row = lax.broadcasted_iota(jnp.int32, (block, block), 0)
    col = lax.broadcasted_iota(jnp.int32, (block, block), 1)
    per = block // dp
    order = (row == (col % per) * dp + col // per).astype(BF16)
    g = arrived_block(block, arrived)
    right_new[...] = STAT_DECAY * right[...] + weight * dot(g, g, 0, 0)
    g = dot(order, g).astype(BF16)
    left_new[...] = STAT_DECAY * left[...] + weight * dot(g, g, 1, 1)
    for pair in range(0, grad.shape[0] // SUB, 2):
        for k in range(wide_chunks):
            wide = grad[pair * SUB : (pair + 2) * SUB, k * LANES : (k + 1) * LANES].astype(F32)
            for side in range(2):
                clipped = clip * wide[side * SUB : (side + 1) * SUB]
                place = pl.ds((pair + side) * SUB * wide_chunks + k, SUB, stride=wide_chunks)
                moment[place, :] = MOMENT_DECAY * second[place, :] + (1.0 - MOMENT_DECAY) * clipped * clipped


def place_kernel(row_blocks, col_blocks, block, owners, owner_lanes, returned, update, held, sems):
    blocks = row_blocks * col_blocks
    tiles = jnp.sum(returned[:, :, FOLDS * block :].astype(F32), axis=1)
    adam_sq = jnp.sum(tiles, axis=0, keepdims=True)[:, :blocks]
    slot = lax.broadcasted_iota(jnp.int32, (tiles.shape[0], blocks), 0)
    norms = jnp.where(owner_lanes[...] == slot, tiles[:, blocks : blocks + 1], 0.0)
    norm_sq = jnp.sum(norms, axis=0, keepdims=True)
    ratio = jnp.sqrt(adam_sq) / jnp.sqrt(norm_sq + NORM_EPS)
    copies = []
    for pair in range(row_blocks // 2):
        for col in range(col_blocks):
            rows = []
            for side in range(2):
                b = (2 * pair + side) * col_blocks + col
                rows.append(ratio[:, b : b + 1] * unfold(returned[pl.ds(owners[b], 1)], block)[0])
            here = slice(pair * 2 * SUB, (pair + 1) * 2 * SUB)
            held[here, col * block : (col + 1) * block] = jnp.concatenate(rows, axis=0).astype(BF16)
        span = pl.ds(pair * 2 * SUB, 2 * SUB)
        copies.append(pltpu.make_async_copy(held.at[span], update.at[span], sems.at[pair]))
        copies[-1].start()
    for copy in copies:
        copy.wait()


def on_device(gradient, second_moment, left_stat, right_stat, left_root, right_root, owner_table):
    dp = lax.axis_size("dp")
    experts = lax.axis_size("expert")
    _, local_rows, _, width = gradient.shape
    block = left_stat.shape[-1]
    row_blocks = local_rows // SUB
    col_blocks = width // block
    limit = math.sqrt(experts * local_rows * dp * width)
    grid = (row_blocks, col_blocks, block)
    grad = gradient.reshape(local_rows, width)
    second = second_moment.reshape(local_rows * width // LANES, LANES)
    owners = owner_table[0]
    packed = jax.ShapeDtypeStruct((dp, ROWS, FOLDS * block + LANES), BF16)
    square = functools.partial(jax.ShapeDtypeStruct, (block, block))
    line = jax.ShapeDtypeStruct((1, LANES), F32)
    cube = 2 * block**3
    area = block * block

    def exchange(x):
        return lax.all_to_all(x, "dp", split_axis=0, concat_axis=0, tiled=True)

    tail = pl.BlockSpec((dp, ROWS, LANES), lambda _: (0, 0, FOLDS * block // LANES))
    pairs = row_blocks // 2
    outgoing = call(
        functools.partial(pack_kernel, *grid), packed, [hbm(), hbm()], hbm(), "pack", moved=4 * area,
        scratch_shapes=[
            pltpu.SMEM(owner_table.shape, jnp.int32),
            pltpu.VMEM(grad.shape, BF16),
            pltpu.VMEM(packed.shape, BF16),
            pltpu.SemaphoreType.DMA((pairs + 1,)),
            pltpu.SemaphoreType.DMA((2,)),
        ],
        limit=PACK_LIMIT,
    )(owner_table, grad)
    arrived = exchange(outgoing)
    pair_of = jax.ShapeDtypeStruct((2, block, block), BF16)
    l_parts, r_parts = call(
        functools.partial(roots_kernel, dp), (pair_of,) * 2, [vmem()] * 2, (vmem(),) * 2, "roots",
        flops=4 * cube, moved=16 * area,
    )(left_root[0, 0], right_root[0, 0])
    sq_a = call(sum_kernel, line, [tail], vmem(), "norm", moved=area, grid=(1,))(arrived)
    sq_b = lax.ppermute(sq_a, "expert", [(j, j ^ 1) for j in range(experts)])
    half = call(
        functools.partial(left_kernel, block), square(F32), [vmem()] * 2, vmem(), "left",
        flops=2 * cube, moved=12 * area,
    )(l_parts, arrived)
    sq_a = sq_a + sq_b
    sq_b = lax.ppermute(sq_a, "expert", [(j, j ^ 3) for j in range(experts)])
    ready, norm = call(
        right_kernel, (packed, jax.ShapeDtypeStruct((SUB, LANES), F32)), [vmem()] * 2, (vmem(),) * 2, "right",
        flops=3 * cube, moved=10 * area,
    )(half, r_parts)
    ready = call(
        functools.partial(adam_kernel, limit, *grid), packed,
        [vmem()] * 5 + [pl.BlockSpec(memory_space=pl.ANY)], tail, "adam",
        moved=8 * area,
        scratch_shapes=[pltpu.VMEM((LANES, LANES), F32)],
        input_output_aliases={5: 0},
        grid=(1,),
    )(grad, second, sq_a, sq_b, norm, ready)
    returned = exchange(ready)
    left_new, right_new, moment = call(
        functools.partial(finish_kernel, limit, dp, block, width // LANES),
        (square(F32), square(F32), jax.ShapeDtypeStruct(second.shape, F32)),
        [vmem()] * 7, (vmem(),) * 3, "finish",
        flops=3 * cube, moved=28 * area,
    )(arrived, sq_a, sq_b, left_stat[0, 0], right_stat[0, 0], grad, second)
    update = call(
        functools.partial(place_kernel, *grid),
        jax.ShapeDtypeStruct((local_rows, width), BF16),
        [smem(), vmem(), vmem()], hbm(), "place",
        moved=4 * area,
        scratch_shapes=[pltpu.VMEM(grad.shape, BF16), pltpu.SemaphoreType.DMA((pairs,))],
    )(owners, owner_table, returned)
    return (
        update.reshape(gradient.shape),
        moment.reshape(second_moment.shape),
        left_new[None, None],
        right_new[None, None],
    )


def solution(mesh):
    rows = P("expert", None, "dp", None)
    slots = P("expert", "dp", None, None)
    return jax.shard_map(
        on_device,
        mesh=mesh,
        in_specs=(rows, rows, slots, slots, slots, slots, P("expert", None)),
        out_specs=(rows, rows, slots, slots),
        check_vma=False,
    )
```

```python
import functools
import math

import jax
import jax.numpy as jnp
from jax import lax
from jax.experimental import pallas as pl
from jax.experimental.pallas import tpu as pltpu
from jax.sharding import PartitionSpec as P

STAT_DECAY = 0.9
MOMENT_DECAY = 0.99
ADAM_EPS = 1e-08
NORM_EPS = 1e-06
LANES = 128
SUB = 8
ROWS = 2
FOLDS = SUB // ROWS
F32 = jnp.float32
BF16 = jnp.bfloat16
VMEM_LIMIT = 48 * 1024 * 1024
PACK_LIMIT = 64 * 1024 * 1024 - 256 * 1024


def call(body, out_shape, in_specs, out_specs, name, flops=0, moved=0, limit=VMEM_LIMIT, **kw):
    return pl.pallas_call(
        body,
        out_shape=out_shape,
        in_specs=in_specs,
        out_specs=out_specs,
        name=name,
        compiler_params=pltpu.CompilerParams(vmem_limit_bytes=limit),
        cost_estimate=pl.CostEstimate(flops=flops, bytes_accessed=moved, transcendentals=0),
        **kw,
    )


def vmem():
    return pl.BlockSpec(memory_space=pltpu.VMEM)


def smem():
    return pl.BlockSpec(memory_space=pltpu.SMEM)


def hbm():
    return pl.BlockSpec(memory_space=pltpu.HBM)


def dot(a, b, ca=1, cb=0):
    return lax.dot_general(a, b, (((ca,), (cb,)), ((), ())), preferred_element_type=F32)


def split2(x):
    high = x.astype(BF16)
    return high, (x - high.astype(F32)).astype(BF16)


def spread(x):
    high = x.astype(BF16).astype(F32)
    row = lax.broadcasted_iota(jnp.int32, x.shape, 0)
    return jnp.where(row == 0, high, x - high).astype(BF16)


def fold(x):
    return jnp.concatenate([x[:, i * ROWS : (i + 1) * ROWS] for i in range(FOLDS)], axis=2).astype(BF16)


def unfold(x, block):
    return jnp.concatenate([x[:, :, i * block : (i + 1) * block].astype(F32) for i in range(FOLDS)], axis=1)


def clip_of(grad_sq, limit):
    return limit / jnp.maximum(jnp.sqrt(grad_sq), limit)


def pack_kernel(row_blocks, col_blocks, block, table, grad, out, owners, held, ready, sems, out_sems):
    rows = 2 * SUB
    place = pltpu.make_async_copy(table, owners, sems.at[row_blocks // 2])
    place.start()
    copies = []
    for pair in range(row_blocks // 2):
        span = pl.ds(pair * rows, rows)
        copies.append(pltpu.make_async_copy(grad.at[span], held.at[span], sems.at[pair]))
        copies[-1].start()
    place.wait()
    total = jnp.zeros((SUB, block), F32)
    for pair, copy in enumerate(copies):
        copy.wait()
        for col in range(col_blocks):
            wide = held[pair * rows : (pair + 1) * rows, col * block : (col + 1) * block].astype(F32)
            for side in range(2):
                piece = wide[side * SUB : (side + 1) * SUB]
                total += piece * piece
                slot = owners[0, (2 * pair + side) * col_blocks + col]
                at = pair * rows + side * SUB
                for i in range(FOLDS):
                    ready[slot, :, i * block : (i + 1) * block] = held[
                        at + i * ROWS : at + (i + 1) * ROWS, col * block : (col + 1) * block
                    ]
                pltpu.make_async_copy(
                    ready.at[slot, :, : FOLDS * block], out.at[slot, :, : FOLDS * block], out_sems.at[0]
                ).start()
    tile = jnp.broadcast_to(jnp.sum(total, keepdims=True), (ROWS, LANES))
    ready[:, :, FOLDS * block :] = jnp.broadcast_to(spread(tile)[None], (ready.shape[0], ROWS, LANES))
    tails = pltpu.make_async_copy(ready.at[:, :, FOLDS * block :], out.at[:, :, FOLDS * block :], out_sems.at[1])
    tails.start()
    pltpu.make_async_copy(ready.at[:, :, : FOLDS * block], out.at[:, :, : FOLDS * block], out_sems.at[0]).wait()
    tails.wait()


def sum_kernel(tiles, out):
    wide = jnp.sum(tiles[...].astype(F32), axis=0)
    out[...] = jnp.sum(wide, axis=0, keepdims=True)


def roots_kernel(dp, left, right, l_parts, r_parts):
    n = left.shape[0]
    row = lax.broadcasted_iota(jnp.int32, (n, n), 0)
    col = lax.broadcasted_iota(jnp.int32, (n, n), 1)
    per = n // dp
    order = (col == (row % per) * dp + row // per).astype(BF16)
    for i, part in enumerate(split2(left[...])):
        rows = dot(order, part).astype(BF16)
        l_parts[i] = dot(rows, order, 1, 1).astype(BF16)
    r_parts[0], r_parts[1] = split2(right[...])


def arrived_block(block, arrived):
    return unfold(arrived, block).reshape(block, block).astype(BF16)


def left_kernel(block, l_parts, arrived, half):
    g = arrived_block(block, arrived)
    half[...] = dot(l_parts[0], g) + dot(l_parts[1], g)


def right_kernel(half, r_parts, out, norm):
    block = half.shape[1]
    high, low = split2(half[...])
    full = dot(high, r_parts[0]) + dot(high, r_parts[1]) + dot(low, r_parts[0])
    norm[...] = jnp.broadcast_to(jnp.sum(full * full, keepdims=True), norm.shape)
    out[:, :, : FOLDS * block] = fold(full.reshape(out.shape[0], SUB, block))


def adam_kernel(limit, row_blocks, col_blocks, block, grad, second, sq_0, sq_1, sq_2, sq_3, norm, _, tail, parts):
    clip = clip_of((sq_0[...] + sq_1[...]) + (sq_2[...] + sq_3[...]), limit)
    chunks = block // LANES
    wide_chunks = col_blocks * chunks
    parts[...] = jnp.zeros_like(parts)
    for pair in range(0, row_blocks, 2):
        for col in range(col_blocks):
            sums = [jnp.zeros((SUB, LANES), F32) for _ in range(2)]
            for chunk in range(chunks):
                k = col * chunks + chunk
                wide = grad[pair * SUB : (pair + 2) * SUB, k * LANES : (k + 1) * LANES].astype(F32)
                for side in range(2):
                    clipped = clip * wide[side * SUB : (side + 1) * SUB]
                    square = clipped * clipped
                    place = pl.ds((pair + side) * SUB * wide_chunks + k, SUB, stride=wide_chunks)
                    new = MOMENT_DECAY * second[place, :] + (1.0 - MOMENT_DECAY) * square
                    below = new * lax.rsqrt(new) + ADAM_EPS
                    sums[side] += square / (below * below)
            for side in range(2):
                b = (pair + side) * col_blocks + col
                parts[b : b + 1, :] = jnp.sum(sums[side], axis=0, keepdims=True)
    sums = lax.dot_general(
        jnp.ones((SUB, LANES), F32),
        parts[...],
        (((1,), (1,)), ((), ())),
        precision=lax.Precision.HIGHEST,
        preferred_element_type=F32,
    )
    lane = lax.broadcasted_iota(jnp.int32, (ROWS, LANES), 1)
    tile = jnp.where(lane == row_blocks * col_blocks, norm[:ROWS], sums[:ROWS])
    tail[...] = jnp.broadcast_to(spread(tile)[None], tail.shape)


def finish_kernel(limit, dp, block, wide_chunks, arrived, sq_0, sq_1, sq_2, sq_3, left, right, grad, second, left_new, right_new, moment):
    clip = clip_of((sq_0[...] + sq_1[...]) + (sq_2[...] + sq_3[...]), limit)
    weight = (1.0 - STAT_DECAY) * clip[:, :1] * clip[:, :1] / block
    row = lax.broadcasted_iota(jnp.int32, (block, block), 0)
    col = lax.broadcasted_iota(jnp.int32, (block, block), 1)
    per = block // dp
    order = (row == (col % per) * dp + col // per).astype(BF16)
    g = arrived_block(block, arrived)
    right_new[...] = STAT_DECAY * right[...] + weight * dot(g, g, 0, 0)
    g = dot(order, g).astype(BF16)
    left_new[...] = STAT_DECAY * left[...] + weight * dot(g, g, 1, 1)
    for pair in range(0, grad.shape[0] // SUB, 2):
        for k in range(wide_chunks):
            wide = grad[pair * SUB : (pair + 2) * SUB, k * LANES : (k + 1) * LANES].astype(F32)
            for side in range(2):
                clipped = clip * wide[side * SUB : (side + 1) * SUB]
                place = pl.ds((pair + side) * SUB * wide_chunks + k, SUB, stride=wide_chunks)
                moment[place, :] = MOMENT_DECAY * second[place, :] + (1.0 - MOMENT_DECAY) * clipped * clipped


def place_kernel(row_blocks, col_blocks, block, table, owner_lanes, returned, update, owners, held, sems):
    placing = pltpu.make_async_copy(table, owners, sems.at[row_blocks // 2])
    placing.start()
    blocks = row_blocks * col_blocks
    tiles = jnp.sum(returned[:, :, FOLDS * block :].astype(F32), axis=1)
    adam_sq = jnp.sum(tiles, axis=0, keepdims=True)[:, :blocks]
    slot = lax.broadcasted_iota(jnp.int32, (tiles.shape[0], blocks), 0)
    norms = jnp.where(owner_lanes[...] == slot, tiles[:, blocks : blocks + 1], 0.0)
    norm_sq = jnp.sum(norms, axis=0, keepdims=True)
    ratio = jnp.sqrt(adam_sq) / jnp.sqrt(norm_sq + NORM_EPS)
    placing.wait()
    copies = []
    for pair in range(row_blocks // 2):
        for col in range(col_blocks):
            rows = []
            for side in range(2):
                b = (2 * pair + side) * col_blocks + col
                rows.append(ratio[:, b : b + 1] * unfold(returned[pl.ds(owners[0, b], 1)], block)[0])
            here = slice(pair * 2 * SUB, (pair + 1) * 2 * SUB)
            held[here, col * block : (col + 1) * block] = jnp.concatenate(rows, axis=0).astype(BF16)
        span = pl.ds(pair * 2 * SUB, 2 * SUB)
        copies.append(pltpu.make_async_copy(held.at[span], update.at[span], sems.at[pair]))
        copies[-1].start()
    for copy in copies:
        copy.wait()


def on_device(gradient, second_moment, left_stat, right_stat, left_root, right_root, owner_table):
    dp = lax.axis_size("dp")
    experts = lax.axis_size("expert")
    _, local_rows, _, width = gradient.shape
    block = left_stat.shape[-1]
    row_blocks = local_rows // SUB
    col_blocks = width // block
    limit = math.sqrt(experts * local_rows * dp * width)
    grid = (row_blocks, col_blocks, block)
    grad = gradient.reshape(local_rows, width)
    second = second_moment.reshape(local_rows * width // LANES, LANES)
    owners = owner_table[0]
    packed = jax.ShapeDtypeStruct((dp, ROWS, FOLDS * block + LANES), BF16)
    square = functools.partial(jax.ShapeDtypeStruct, (block, block))
    line = jax.ShapeDtypeStruct((1, LANES), F32)
    cube = 2 * block**3
    area = block * block

    def exchange(x):
        return lax.all_to_all(x, "dp", split_axis=0, concat_axis=0, tiled=True)

    tail = pl.BlockSpec((dp, ROWS, LANES), lambda _: (0, 0, FOLDS * block // LANES))
    pairs = row_blocks // 2
    def swap(x, step):
        pairs = [(i * experts + j, (i ^ 1) * experts + (j ^ step)) for i in range(dp) for j in range(experts)]
        return lax.ppermute(x, ("dp", "expert"), pairs)

    outgoing = call(
        functools.partial(pack_kernel, *grid), packed, [hbm(), hbm()], hbm(), "pack", moved=4 * area,
        scratch_shapes=[
            pltpu.SMEM(owner_table.shape, jnp.int32),
            pltpu.VMEM(grad.shape, BF16),
            pltpu.VMEM(packed.shape, BF16),
            pltpu.SemaphoreType.DMA((pairs + 1,)),
            pltpu.SemaphoreType.DMA((2,)),
        ],
        limit=PACK_LIMIT,
    )(owner_table, grad)
    arrived = exchange(outgoing)
    pair_of = jax.ShapeDtypeStruct((2, block, block), BF16)
    l_parts, r_parts = call(
        functools.partial(roots_kernel, dp), (pair_of,) * 2, [vmem()] * 2, (vmem(),) * 2, "roots",
        flops=4 * cube, moved=16 * area,
    )(left_root[0, 0], right_root[0, 0])
    sq_a = call(sum_kernel, line, [tail], vmem(), "norm", moved=area, grid=(1,))(arrived)
    sqs = [sq_a] + [swap(sq_a, step) for step in range(1, experts)]
    half = call(
        functools.partial(left_kernel, block), square(F32), [vmem()] * 2, vmem(), "left",
        flops=2 * cube, moved=12 * area,
    )(l_parts, arrived)
    ready, norm = call(
        right_kernel, (packed, jax.ShapeDtypeStruct((SUB, LANES), F32)), [vmem()] * 2, (vmem(),) * 2, "right",
        flops=3 * cube, moved=10 * area,
    )(half, r_parts)
    ready = call(
        functools.partial(adam_kernel, limit, *grid), packed,
        [vmem()] * 7 + [pl.BlockSpec(memory_space=pl.ANY)], tail, "adam",
        moved=8 * area,
        scratch_shapes=[pltpu.VMEM((LANES, LANES), F32)],
        input_output_aliases={7: 0},
        grid=(1,),
    )(grad, second, *sqs, norm, ready)
    returned = exchange(ready)
    left_new, right_new, moment = call(
        functools.partial(finish_kernel, limit, dp, block, width // LANES),
        (square(F32), square(F32), jax.ShapeDtypeStruct(second.shape, F32)),
        [vmem()] * 9, (vmem(),) * 3, "finish",
        flops=3 * cube, moved=28 * area,
    )(arrived, *sqs, left_stat[0, 0], right_stat[0, 0], grad, second)
    update = call(
        functools.partial(place_kernel, *grid),
        jax.ShapeDtypeStruct((local_rows, width), BF16),
        [hbm(), vmem(), vmem()], hbm(), "place",
        moved=4 * area,
        scratch_shapes=[
            pltpu.SMEM(owner_table.shape, jnp.int32),
            pltpu.VMEM(grad.shape, BF16),
            pltpu.SemaphoreType.DMA((pairs + 1,)),
        ],
    )(owner_table, owner_table, returned)
    return (
        update.reshape(gradient.shape),
        moment.reshape(second_moment.shape),
        left_new[None, None],
        right_new[None, None],
    )


def solution(mesh):
    rows = P("expert", None, "dp", None)
    slots = P("expert", "dp", None, None)
    return jax.shard_map(
        on_device,
        mesh=mesh,
        in_specs=(rows, rows, slots, slots, slots, slots, P("expert", None)),
        out_specs=(rows, rows, slots, slots),
        check_vma=False,
    )
```

```python
import functools
import math

import jax
import jax.numpy as jnp
from jax import lax
from jax.experimental import pallas as pl
from jax.experimental.pallas import tpu as pltpu
from jax.sharding import PartitionSpec as P

STAT_DECAY = 0.9
MOMENT_DECAY = 0.99
ADAM_EPS = 1e-08
NORM_EPS = 1e-06
LANES = 128
SUB = 8
ROWS = 2
FOLDS = SUB // ROWS
F32 = jnp.float32
BF16 = jnp.bfloat16
VMEM_LIMIT = 48 * 1024 * 1024
PACK_LIMIT = 64 * 1024 * 1024 - 256 * 1024


def call(body, out_shape, in_specs, out_specs, name, flops=0, moved=0, limit=VMEM_LIMIT, **kw):
    return pl.pallas_call(
        body,
        out_shape=out_shape,
        in_specs=in_specs,
        out_specs=out_specs,
        name=name,
        compiler_params=pltpu.CompilerParams(vmem_limit_bytes=limit),
        cost_estimate=pl.CostEstimate(flops=flops, bytes_accessed=moved, transcendentals=0),
        **kw,
    )


def vmem():
    return pl.BlockSpec(memory_space=pltpu.VMEM)


def smem():
    return pl.BlockSpec(memory_space=pltpu.SMEM)


def hbm():
    return pl.BlockSpec(memory_space=pltpu.HBM)


def dot(a, b, ca=1, cb=0):
    return lax.dot_general(a, b, (((ca,), (cb,)), ((), ())), preferred_element_type=F32)


def split2(x):
    high = x.astype(BF16)
    return high, (x - high.astype(F32)).astype(BF16)


def spread(x):
    high = x.astype(BF16).astype(F32)
    row = lax.broadcasted_iota(jnp.int32, x.shape, 0)
    return jnp.where(row == 0, high, x - high).astype(BF16)


def fold(x):
    return jnp.concatenate([x[:, i * ROWS : (i + 1) * ROWS] for i in range(FOLDS)], axis=2).astype(BF16)


def unfold(x, block):
    return jnp.concatenate([x[:, :, i * block : (i + 1) * block] for i in range(FOLDS)], axis=1).astype(F32)


def clip_of(grad_sq, limit):
    return limit / jnp.maximum(jnp.sqrt(grad_sq), limit)


def pack_kernel(row_blocks, col_blocks, block, table, grad, out, owners, held, ready, sems, out_sems):
    rows = 2 * SUB
    place = pltpu.make_async_copy(table, owners, sems.at[row_blocks // 2])
    place.start()
    copies = []
    for pair in range(row_blocks // 2):
        span = pl.ds(pair * rows, rows)
        copies.append(pltpu.make_async_copy(grad.at[span], held.at[span], sems.at[pair]))
        copies[-1].start()
    place.wait()
    total = jnp.zeros((SUB, block), F32)
    for pair, copy in enumerate(copies):
        copy.wait()
        for col in range(col_blocks):
            wide = held[pair * rows : (pair + 1) * rows, col * block : (col + 1) * block].astype(F32)
            for side in range(2):
                piece = wide[side * SUB : (side + 1) * SUB]
                total += piece * piece
                slot = owners[0, (2 * pair + side) * col_blocks + col]
                at = pair * rows + side * SUB
                for i in range(FOLDS):
                    ready[slot, :, i * block : (i + 1) * block] = held[
                        at + i * ROWS : at + (i + 1) * ROWS, col * block : (col + 1) * block
                    ]
                pltpu.make_async_copy(
                    ready.at[slot, :, : FOLDS * block], out.at[slot, :, : FOLDS * block], out_sems.at[0]
                ).start()
    tile = jnp.broadcast_to(jnp.sum(total, keepdims=True), (ROWS, LANES))
    ready[:, :, FOLDS * block :] = jnp.broadcast_to(spread(tile)[None], (ready.shape[0], ROWS, LANES))
    tails = pltpu.make_async_copy(ready.at[:, :, FOLDS * block :], out.at[:, :, FOLDS * block :], out_sems.at[1])
    tails.start()
    pltpu.make_async_copy(ready.at[:, :, : FOLDS * block], out.at[:, :, : FOLDS * block], out_sems.at[0]).wait()
    tails.wait()


def sum_kernel(tiles, out):
    wide = jnp.sum(tiles[...].astype(F32), axis=0)
    out[...] = jnp.sum(wide, axis=0, keepdims=True)


def roots_kernel(dp, left, right, l_parts, r_parts):
    n = left.shape[0]
    row = lax.broadcasted_iota(jnp.int32, (n, n), 0)
    col = lax.broadcasted_iota(jnp.int32, (n, n), 1)
    per = n // dp
    order = (col == (row % per) * dp + row // per).astype(BF16)
    for i, part in enumerate(split2(left[...])):
        rows = dot(order, part).astype(BF16)
        l_parts[i] = dot(rows, order, 1, 1).astype(BF16)
    r_parts[0], r_parts[1] = split2(right[...])


def arrived_block(block, arrived):
    return unfold(arrived, block).reshape(block, block).astype(BF16)


def left_kernel(block, l_parts, arrived, half):
    g = arrived_block(block, arrived)
    half[...] = dot(l_parts[0], g) + dot(l_parts[1], g)


def right_kernel(half, r_parts, out, norm):
    block = half.shape[1]
    high, low = split2(half[...])
    full = dot(high, r_parts[0]) + dot(high, r_parts[1]) + dot(low, r_parts[0])
    norm[...] = jnp.broadcast_to(jnp.sum(full * full, keepdims=True), norm.shape)
    whole = full.reshape(out.shape[0], SUB, block)
    for i in range(FOLDS):
        out[:, :, i * block : (i + 1) * block] = whole[:, i * ROWS : (i + 1) * ROWS].astype(BF16)


def adam_kernel(limit, row_blocks, col_blocks, block, grad, second, sq_0, sq_1, sq_2, sq_3, norm, data, out, parts, tail, sems):
    body = pltpu.make_async_copy(data, out.at[:, :, : FOLDS * block], sems.at[0])
    body.start()
    clip = clip_of((sq_0[...] + sq_1[...]) + (sq_2[...] + sq_3[...]), limit)
    chunks = block // LANES
    wide_chunks = col_blocks * chunks
    parts[...] = jnp.zeros_like(parts)
    for pair in range(0, row_blocks, 2):
        for col in range(col_blocks):
            sums = [jnp.zeros((SUB, LANES), F32) for _ in range(2)]
            for chunk in range(chunks):
                k = col * chunks + chunk
                wide = grad[pair * SUB : (pair + 2) * SUB, k * LANES : (k + 1) * LANES].astype(F32)
                for side in range(2):
                    clipped = clip * wide[side * SUB : (side + 1) * SUB]
                    square = clipped * clipped
                    place = pl.ds((pair + side) * SUB * wide_chunks + k, SUB, stride=wide_chunks)
                    new = MOMENT_DECAY * second[place, :] + (1.0 - MOMENT_DECAY) * square
                    below = new * lax.rsqrt(new) + ADAM_EPS
                    sums[side] += square / (below * below)
            for side in range(2):
                b = (pair + side) * col_blocks + col
                parts[b : b + 1, :] = jnp.sum(sums[side], axis=0, keepdims=True)
    sums = lax.dot_general(
        jnp.ones((SUB, LANES), F32),
        parts[...],
        (((1,), (1,)), ((), ())),
        precision=lax.Precision.HIGHEST,
        preferred_element_type=F32,
    )
    lane = lax.broadcasted_iota(jnp.int32, (ROWS, LANES), 1)
    tile = jnp.where(lane == row_blocks * col_blocks, norm[:ROWS], sums[:ROWS])
    tail[...] = jnp.broadcast_to(spread(tile)[None], tail.shape)
    end = pltpu.make_async_copy(tail, out.at[:, :, FOLDS * block :], sems.at[1])
    end.start()
    body.wait()
    end.wait()


def finish_kernel(limit, dp, block, wide_chunks, arrived, sq_0, sq_1, sq_2, sq_3, left, right, grad, second, left_new, right_new, moment):
    clip = clip_of((sq_0[...] + sq_1[...]) + (sq_2[...] + sq_3[...]), limit)
    weight = (1.0 - STAT_DECAY) * clip[:, :1] * clip[:, :1] / block
    row = lax.broadcasted_iota(jnp.int32, (block, block), 0)
    col = lax.broadcasted_iota(jnp.int32, (block, block), 1)
    per = block // dp
    order = (row == (col % per) * dp + col // per).astype(BF16)
    g = arrived_block(block, arrived)
    right_new[...] = STAT_DECAY * right[...] + weight * dot(g, g, 0, 0)
    g = dot(order, g).astype(BF16)
    left_new[...] = STAT_DECAY * left[...] + weight * dot(g, g, 1, 1)
    for pair in range(0, grad.shape[0] // SUB, 2):
        for k in range(wide_chunks):
            wide = grad[pair * SUB : (pair + 2) * SUB, k * LANES : (k + 1) * LANES].astype(F32)
            for side in range(2):
                clipped = clip * wide[side * SUB : (side + 1) * SUB]
                place = pl.ds((pair + side) * SUB * wide_chunks + k, SUB, stride=wide_chunks)
                moment[place, :] = MOMENT_DECAY * second[place, :] + (1.0 - MOMENT_DECAY) * clipped * clipped


def place_kernel(row_blocks, col_blocks, block, table, owner_lanes, returned, update, owners, held, sems):
    placing = pltpu.make_async_copy(table, owners, sems.at[row_blocks // 2])
    placing.start()
    blocks = row_blocks * col_blocks
    tiles = jnp.sum(returned[:, :, FOLDS * block :].astype(F32), axis=1)
    adam_sq = jnp.sum(tiles, axis=0, keepdims=True)[:, :blocks]
    slot = lax.broadcasted_iota(jnp.int32, (tiles.shape[0], blocks), 0)
    norms = jnp.where(owner_lanes[...] == slot, tiles[:, blocks : blocks + 1], 0.0)
    norm_sq = jnp.sum(norms, axis=0, keepdims=True)
    ratio = jnp.sqrt(adam_sq) / jnp.sqrt(norm_sq + NORM_EPS)
    placing.wait()
    copies = []
    for pair in range(row_blocks // 2):
        for col in range(col_blocks):
            rows = []
            for side in range(2):
                b = (2 * pair + side) * col_blocks + col
                rows.append(ratio[:, b : b + 1] * unfold(returned[pl.ds(owners[0, b], 1)], block)[0])
            here = slice(pair * 2 * SUB, (pair + 1) * 2 * SUB)
            held[here, col * block : (col + 1) * block] = jnp.concatenate(rows, axis=0).astype(BF16)
        span = pl.ds(pair * 2 * SUB, 2 * SUB)
        copies.append(pltpu.make_async_copy(held.at[span], update.at[span], sems.at[pair]))
        copies[-1].start()
    for copy in copies:
        copy.wait()


def on_device(gradient, second_moment, left_stat, right_stat, left_root, right_root, owner_table):
    dp = lax.axis_size("dp")
    experts = lax.axis_size("expert")
    _, local_rows, _, width = gradient.shape
    block = left_stat.shape[-1]
    row_blocks = local_rows // SUB
    col_blocks = width // block
    limit = math.sqrt(experts * local_rows * dp * width)
    grid = (row_blocks, col_blocks, block)
    grad = gradient.reshape(local_rows, width)
    second = second_moment.reshape(local_rows * width // LANES, LANES)
    owners = owner_table[0]
    packed = jax.ShapeDtypeStruct((dp, ROWS, FOLDS * block + LANES), BF16)
    square = functools.partial(jax.ShapeDtypeStruct, (block, block))
    line = jax.ShapeDtypeStruct((1, LANES), F32)
    cube = 2 * block**3
    area = block * block

    def exchange(x):
        return lax.all_to_all(x, "dp", split_axis=0, concat_axis=0, tiled=True)

    tail = pl.BlockSpec((dp, ROWS, LANES), lambda _: (0, 0, FOLDS * block // LANES))
    pairs = row_blocks // 2
    def swap(x, step):
        pairs = [(i * experts + j, (i ^ 1) * experts + (j ^ step)) for i in range(dp) for j in range(experts)]
        return lax.ppermute(x, ("dp", "expert"), pairs)

    outgoing = call(
        functools.partial(pack_kernel, *grid), packed, [hbm(), hbm()], hbm(), "pack", moved=4 * area,
        scratch_shapes=[
            pltpu.SMEM(owner_table.shape, jnp.int32),
            pltpu.VMEM(grad.shape, BF16),
            pltpu.VMEM(packed.shape, BF16),
            pltpu.SemaphoreType.DMA((pairs + 1,)),
            pltpu.SemaphoreType.DMA((2,)),
        ],
        limit=PACK_LIMIT,
    )(owner_table, grad)
    arrived = exchange(outgoing)
    pair_of = jax.ShapeDtypeStruct((2, block, block), BF16)
    l_parts, r_parts = call(
        functools.partial(roots_kernel, dp), (pair_of,) * 2, [vmem()] * 2, (vmem(),) * 2, "roots",
        flops=4 * cube, moved=16 * area,
    )(left_root[0, 0], right_root[0, 0])
    sq_a = call(sum_kernel, line, [tail], vmem(), "norm", moved=area, grid=(1,))(arrived)
    sqs = [sq_a] + [swap(sq_a, step) for step in range(1, experts)]
    half = call(
        functools.partial(left_kernel, block), square(F32), [vmem()] * 2, vmem(), "left",
        flops=2 * cube, moved=12 * area,
    )(l_parts, arrived)
    ready, norm = call(
        right_kernel,
        (jax.ShapeDtypeStruct((dp, ROWS, FOLDS * block), BF16), jax.ShapeDtypeStruct((SUB, LANES), F32)),
        [vmem()] * 2, (vmem(),) * 2, "right",
        flops=3 * cube, moved=10 * area,
    )(half, r_parts)
    ready = call(
        functools.partial(adam_kernel, limit, *grid), packed, [vmem()] * 8, hbm(), "adam",
        moved=10 * area,
        scratch_shapes=[
            pltpu.VMEM((LANES, LANES), F32),
            pltpu.VMEM((dp, ROWS, LANES), BF16),
            pltpu.SemaphoreType.DMA((2,)),
        ],
    )(grad, second, *sqs, norm, ready)
    returned = exchange(ready)
    left_new, right_new, moment = call(
        functools.partial(finish_kernel, limit, dp, block, width // LANES),
        (square(F32), square(F32), jax.ShapeDtypeStruct(second.shape, F32)),
        [vmem()] * 9, (vmem(),) * 3, "finish",
        flops=3 * cube, moved=28 * area,
    )(arrived, *sqs, left_stat[0, 0], right_stat[0, 0], grad, second)
    update = call(
        functools.partial(place_kernel, *grid),
        jax.ShapeDtypeStruct((local_rows, width), BF16),
        [hbm(), vmem(), vmem()], hbm(), "place",
        moved=4 * area,
        scratch_shapes=[
            pltpu.SMEM(owner_table.shape, jnp.int32),
            pltpu.VMEM(grad.shape, BF16),
            pltpu.SemaphoreType.DMA((pairs + 1,)),
        ],
    )(owner_table, owner_table, returned)
    return (
        update.reshape(gradient.shape),
        moment.reshape(second_moment.shape),
        left_new[None, None],
        right_new[None, None],
    )


def solution(mesh):
    rows = P("expert", None, "dp", None)
    slots = P("expert", "dp", None, None)
    return jax.shard_map(
        on_device,
        mesh=mesh,
        in_specs=(rows, rows, slots, slots, slots, slots, P("expert", None)),
        out_specs=(rows, rows, slots, slots),
        check_vma=False,
    )
```
